32 devices in a mesh: dp: 8 (over z, x), tensor: 4 (over y, core).
Axes of the slice: x: 2, y: 2, z: 4, core: 2. Of those that a mesh axis runs over, the one named last changes fastest.
Arguments:
- block_input: float32 [2048, 768], P('dp'), may hold values from -6 to 6
- first_gain: float32 [768], replicated, may hold values from 0.5 to 1.5
- first_shift: float32 [768], replicated, may hold values from -3 to 3
- input_weight: bfloat16 [768, 2304], P(None, 'tensor'), may hold values from -1.5 to 1.5
- input_bias: float32 [1536], P('tensor'), may hold values from -3 to 3
- output_weight: bfloat16 [768, 768], P('tensor'), may hold values from -0.875 to 0.875
- output_bias: float32 [768], replicated, may hold values from -3 to 3
- second_gain: float32 [768], replicated, may hold values from 0.5 to 1.5
- second_shift: float32 [768], replicated, may hold values from -3 to 3
- expand_weight: bfloat16 [768, 3072], P(None, 'tensor'), may hold values from -0.21875 to 0.21875
- expand_bias: float32 [3072], P('tensor'), may hold values from -3 to 3
- reduce_weight: bfloat16 [3072, 768], P('tensor'), may hold values from -0.109375 to 0.109375
- reduce_bias: float32 [768], replicated, may hold values from -3 to 3
- output_grad: float32 [2048, 768], P('dp'), may hold values from -6 to 6
- segment_ids: int32 [2048], replicated, may hold values from 0 to 15, never falling along the last dimension, each value on 1 to 256 neighbouring positions
- shard_counts: int32 [8], replicated, may hold values from 128 to 256, as said below
Outputs:
- block_output: float32 [2048, 768], P(('dp', 'tensor'))
- input_grad: float32 [2048, 768], P(('dp', 'tensor'))
- first_gain_grad: float32 [768], P('dp')
- first_shift_grad: float32 [768], P('dp')
- input_weight_grad: float32 [768, 2304], P('dp', 'tensor')
- input_bias_grad: float32 [1536], P(('tensor', 'dp'))
- output_weight_grad: float32 [768, 768], P('tensor', 'dp')
- output_bias_grad: float32 [768], P('dp')
- second_gain_grad: float32 [768], P('dp')
- second_shift_grad: float32 [768], P('dp')
- expand_weight_grad: float32 [768, 3072], P('dp', 'tensor')
- expand_bias_grad: float32 [3072], P(('tensor', 'dp'))
- reduce_weight_grad: float32 [3072, 768], P('tensor', 'dp')
- reduce_bias_grad: float32 [768], P('dp')
The draws below stay inside these ranges and needn't reach their ends.
Inputs may be any that keep to these rules, and one draw needn't show every extreme that they name: `segment_ids`: never falling along the token slots; one sequence covers at most 256 consecutive slots, dead slots included, and some sequence covers exactly 256. `shard_counts`: the live slots of a shard are its first ones; some shard is full in every draw.
All inputs are finite; a program needn't handle non-finite values.
Results may differ from the reference program's by a relative error of at most 0.0092.
Values may be sent and summed in bfloat16 or wider, within the bound.
A program may use at most 64 MiB of HBM per device.

```python
import math
import jax
import jax.numpy as jnp
import numpy as np
from jax import lax

D = 768
HEADS = 12
HEAD_DIM = 64
FF = 3072
TOK_DEV = 256
MAXLEN = 256
SHARDS = 8
TOKENS = 2048
SEGMENTS = 16


def draw_shard_counts(key, part):
    first_key = jax.random.fold_in(key, 11)
    second_key = jax.random.fold_in(key, 12)
    drawn = jax.random.randint(first_key, (SHARDS,), TOK_DEV // 2, TOK_DEV + 1)
    full_slot = jax.random.randint(second_key, (), 0, SHARDS)
    return jnp.where(jnp.arange(SHARDS) == full_slot, TOK_DEV, drawn).astype(jnp.int32)


def draw_block_input(key, part):
    base_key = jax.random.fold_in(key, 21)
    values = jnp.clip(jax.random.normal(base_key, (TOKENS, D), jnp.float32), -6.0, 6.0)
    return values


def draw_input_weight(key, part):
    weight_key = jax.random.fold_in(key, 31)
    values = jnp.clip(jax.random.normal(weight_key, (D, 3 * D), jnp.float32), -3.0, 3.0) * D ** (-0.5)
    return values.astype(jnp.bfloat16)


def spiked(values, rng, source, target, parts, factor):
    def block_of(axis_at):
        return (jnp.arange(values.shape[axis_at]) // (values.shape[axis_at] // parts)).reshape((-1,) + (1,) * (values.ndim - 1 - axis_at))

    near = jax.random.permutation(rng, parts)[block_of(target)]
    other_side = (block_of(target) + parts // 2) % parts
    return jnp.where((block_of(source) == near) | (block_of(source) == other_side), factor * values, values)


def block_levels(stream_key, dims, split, smallest, high):
    def one(dim, shards_of):
        draws = jax.random.uniform(jax.random.fold_in(jax.random.fold_in(stream_key, 6), dim), (shards_of,), jnp.float32, smallest / len(split), high / len(split))
        return jnp.repeat(jnp.exp(draws), dims[dim] // shards_of).reshape((-1,) + (1,) * (len(dims) - dim - 1))

    gain = one(*split[0])
    for cut in split[1:]:
        gain = gain * one(*cut)
    return gain


def profile(count, total, reach, lean):
    loads = [(1 << 20) // math.isqrt(standing ** lean) + 1 for standing in range(2, count + 1)]
    surplus, counts = total - reach - (count - 1), [1] * (count - 1)
    while surplus > 0:
        candidates = [i for i in range(count - 1) if counts[i] < reach]
        mass, left = sum([loads[i] for i in candidates]), surplus
        for i in candidates:
            extra = min(reach - counts[i], max(1, left * loads[i] // mass), surplus)
            counts[i] = counts[i] + extra
            surplus = surplus - extra
    return np.array([reach] + counts)


def uneven(key, number_of, total, bound, slope):
    if number_of == 2:
        one = jax.random.randint(key, (), max(1, total - bound), min(bound, total - 1) + 1)
        return jnp.stack([one, total - one])
    sizes = jnp.asarray(profile(number_of, total, bound, slope), jnp.int32)
    pairs = (number_of - 1) // 2
    giver, sink = sizes[1:1 + 2 * pairs:2], sizes[2:2 + 2 * pairs:2]
    room = jnp.minimum(giver - 1, bound - sink)
    passed = jax.random.randint(jax.random.fold_in(key, 1), (pairs,), 0, 1 << 20) % (room + 1)
    sizes = sizes.at[1:1 + 2 * pairs:2].set(giver - passed).at[2:2 + 2 * pairs:2].set(sink + passed)
    return sizes[jax.random.permutation(jax.random.fold_in(key, 2), number_of)]


def noise(rng, shape, deviation, reach, cuts=(), kind=jnp.bfloat16):
    values = deviation * jax.random.normal(rng, shape, jnp.float32)
    if cuts:
        values = values * block_levels(rng, shape, cuts, -0.22, 0.18)
    return jnp.clip(values, -reach, reach).astype(kind)


def bell_draw_with(key, extent, scale, reach, split, heavy, kind=jnp.bfloat16):
    values = scale * jax.random.normal(key, extent, jnp.float32)
    if split:
        values = values * block_levels(key, extent, split, -0.22, 0.18)
    return jnp.clip(spiked(values, jax.random.fold_in(key, 3), *heavy), -reach, reach).astype(kind)


def setup_inputs(seed: int = 0) -> dict:
    keys = jax.random.split(jax.random.key(seed), 17)
    block_input = draw_block_input(jax.random.fold_in(keys[16], 71), 0)
    first_gain = jnp.clip(1.0 + 0.1 * jax.random.normal(keys[1], (D,), jnp.float32), 0.5, 1.5)
    first_shift = noise(keys[2], (D,), 0.5, 3.0, (), jnp.float32)
    input_weight = draw_input_weight(jax.random.fold_in(keys[16], 71), 0)
    input_bias = noise(keys[4], (2 * D,), 0.5, 3.0, ((0, 4),), jnp.float32)
    output_weight = noise(keys[5], (D, D), (D // 16) ** -0.5, 0.875, ((0, 4),))
    output_bias = noise(keys[6], (D,), 0.5, 3.0, (), jnp.float32)
    second_gain = jnp.clip(1.0 + 0.1 * jax.random.normal(keys[7], (D,), jnp.float32), 0.5, 1.5)
    second_shift = noise(keys[8], (D,), 0.5, 3.0, (), jnp.float32)
    expand_weight = noise(keys[9], (D, FF), D ** -0.5, 0.21875, ((1, 4),))
    expand_bias = noise(keys[10], (FF,), 0.5, 3.0, ((0, 4),), jnp.float32)
    reduce_weight = noise(keys[11], (FF, D), FF ** -0.5, 0.109375, ((0, 4),))
    reduce_bias = noise(keys[12], (D,), 0.5, 3.0, (), jnp.float32)
    output_grad = bell_draw_with(keys[13], (TOKENS, D), 1.0, 6.0, ((0, 8),), (0, 1, 8, 2.0), jnp.float32)
    segment_ids = jnp.searchsorted(jnp.cumsum(uneven(keys[14], SEGMENTS, TOKENS, MAXLEN, 1)), jnp.arange(TOKENS), side="right").astype(jnp.int32)
    shard_counts = draw_shard_counts(jax.random.fold_in(keys[16], 71), 0)
    return {"block_input": block_input, "first_gain": first_gain, "first_shift": first_shift, "input_weight": input_weight, "input_bias": input_bias, "output_weight": output_weight, "output_bias": output_bias, "second_gain": second_gain, "second_shift": second_shift, "expand_weight": expand_weight, "expand_bias": expand_bias, "reduce_weight": reduce_weight, "reduce_bias": reduce_bias, "output_grad": output_grad, "segment_ids": segment_ids, "shard_counts": shard_counts}


EPSILON = 1e-05
GELU_COEF = 0.7978845608028654
CUBIC = 0.044715

def layer_norm(values_in, gain_row, shift_row):
    centred = values_in - lax.optimization_barrier(jnp.mean(values_in, axis=-1, keepdims=True))
    reciprocal = lax.rsqrt(lax.optimization_barrier(jnp.mean(centred * centred, axis=-1, keepdims=True)) + EPSILON)
    normed = centred * reciprocal
    return (normed * gain_row + shift_row, normed, reciprocal)

def norm_back(grad_in, normed, reciprocal, gain_row):
    scaled = grad_in * gain_row
    spread = scaled - lax.optimization_barrier(jnp.mean(scaled, axis=-1, keepdims=True)) - normed * lax.optimization_barrier(jnp.mean(scaled * normed, axis=-1, keepdims=True))
    return (reciprocal * spread, lax.optimization_barrier(jnp.sum(grad_in * normed, axis=0)), lax.optimization_barrier(jnp.sum(grad_in, axis=0)))

def gelu_parts(pre_act):
    tanh_value = jnp.tanh(GELU_COEF * (pre_act + CUBIC * pre_act * pre_act * pre_act))
    result = 0.5 * pre_act * (1.0 + tanh_value)
    slope_value = 0.5 * (1.0 + tanh_value) + 0.5 * pre_act * (1.0 - tanh_value * tanh_value) * GELU_COEF * (1.0 + 3.0 * CUBIC * pre_act * pre_act)
    return (result, slope_value)

def full_bias(pairs):
    shaped = pairs.reshape(HEADS, 2, HEAD_DIM)
    return jnp.stack([shaped[:, 0], jnp.zeros_like(shaped[:, 0]), shaped[:, 1]], axis=1).reshape(3 * D)

def block_mask(index, segment_ids, shard_counts):
    position = jnp.arange(TOK_DEV, dtype=jnp.int32)
    prior_index = jnp.maximum(index - 1, 0).astype(jnp.int32)
    own_ids = lax.dynamic_slice_in_dim(segment_ids, (index * TOK_DEV).astype(jnp.int32), TOK_DEV)
    prior_ids = lax.dynamic_slice_in_dim(segment_ids, (prior_index * TOK_DEV).astype(jnp.int32), TOK_DEV)
    own_live = position < shard_counts[index]
    prior_live = (position < shard_counts[prior_index]) & (index > 0)
    diagonal = position[None, :] == position[:, None]
    same_own = (own_ids[:, None] == own_ids[None, :]) & (position[None, :] <= position[:, None]) & (own_live[None, :] | diagonal)
    same_prior = (own_ids[:, None] == prior_ids[None, :]) & prior_live[None, :]
    return (jnp.concatenate([same_prior, same_own], axis=1), own_live)

def masked_scores(queries, key_rows, allowed):
    scores = jnp.einsum('qhd,khd->hqk', queries.astype(jnp.float32), key_rows.astype(jnp.float32)) * HEAD_DIM ** (-0.5)
    return jnp.where(allowed[None], scores, -1e+30)

def reference(block_input, first_gain, first_shift, input_weight, input_bias, output_weight, output_bias, second_gain, second_shift, expand_weight, expand_bias, reduce_weight, reduce_bias, output_grad, segment_ids, shard_counts):
    bias_row = full_bias(input_bias)
    blocks_in = block_input.reshape(SHARDS, TOK_DEV, D)
    blocks_grad = output_grad.reshape(SHARDS, TOK_DEV, D)
    score_scale = HEAD_DIM ** (-0.5)
    f32 = jnp.float32
    b16 = jnp.bfloat16

    def project(index):
        block_rows = lax.dynamic_index_in_dim(blocks_in, index, 0, keepdims=False)
        first_out, normed1, recip1 = layer_norm(block_rows, first_gain, first_shift)
        first_in = first_out.astype(b16)
        mixed = (jnp.dot(first_in, input_weight, preferred_element_type=f32) + bias_row).astype(b16)
        return (block_rows, first_in, normed1, recip1, mixed.reshape(TOK_DEV, HEADS, 3, HEAD_DIM))

    def step(carry, index):
        from_next, totals = carry
        block_rows, first_in, normed1, recip1, mixed = project(index)
        prior_mixed = project(jnp.maximum(index - 1, 0).astype(jnp.int32))[4]
        allowed, own_live = block_mask(index, segment_ids, shard_counts)
        live_col = own_live.astype(f32)[:, None]
        queries = mixed[:, :, 0]
        key_rows = jnp.concatenate([prior_mixed[:, :, 1], mixed[:, :, 1]], axis=0)
        value_rows = jnp.concatenate([prior_mixed[:, :, 2], mixed[:, :, 2]], axis=0)
        scores = masked_scores(queries, key_rows, allowed)
        row_top = lax.optimization_barrier(jnp.max(scores, axis=-1, keepdims=True))
        logsum = row_top + jnp.log(lax.optimization_barrier(jnp.sum(jnp.exp(scores - row_top), axis=-1, keepdims=True)))
        soft = jnp.exp(scores - logsum)
        soft16 = soft.astype(b16)
        attended = jnp.einsum('hqk,khd->qhd', soft16.astype(f32), value_rows.astype(f32)).astype(b16).reshape(TOK_DEV, D)
        hidden = block_rows + jnp.dot(attended, output_weight, preferred_element_type=f32) + output_bias
        second_out, normed2, recip2 = layer_norm(hidden, second_gain, second_shift)
        second_in = second_out.astype(b16)
        pre_act = jnp.dot(second_in, expand_weight, preferred_element_type=f32) + expand_bias
        activ, gelu_slope = gelu_parts(pre_act)
        activated = activ.astype(b16)
        block_output = live_col * (hidden + jnp.dot(activated, reduce_weight, preferred_element_type=f32) + reduce_bias)
        grad_y = live_col * lax.dynamic_index_in_dim(blocks_grad, index, 0, keepdims=False)
        grad_y16 = grad_y.astype(b16)
        reduce_weight_grad = jnp.dot(activated.T, grad_y16, preferred_element_type=f32)
        reduce_bias_grad = lax.optimization_barrier(jnp.sum(grad_y, axis=0))
        grad_pre = jnp.dot(grad_y16, reduce_weight.T, preferred_element_type=f32) * gelu_slope
        grad_pre16 = grad_pre.astype(b16)
        expand_weight_grad = jnp.dot(second_in.T, grad_pre16, preferred_element_type=f32)
        expand_bias_grad = lax.optimization_barrier(jnp.sum(grad_pre, axis=0))
        grad_norm2 = jnp.dot(grad_pre16, expand_weight.T, preferred_element_type=f32)
        back2, second_gain_grad, second_shift_grad = norm_back(grad_norm2, normed2, recip2, second_gain)
        grad_hidden = grad_y + back2
        grad_hidden16 = grad_hidden.astype(b16)
        output_weight_grad = jnp.dot(attended.T, grad_hidden16, preferred_element_type=f32)
        output_bias_grad = lax.optimization_barrier(jnp.sum(grad_hidden, axis=0))
        grad_att = jnp.dot(grad_hidden16, output_weight.T, preferred_element_type=f32).astype(b16).reshape(TOK_DEV, HEADS, HEAD_DIM)
        grad_soft = jnp.einsum('qhd,khd->hqk', grad_att.astype(f32), value_rows.astype(f32))
        delta = lax.optimization_barrier(jnp.sum(soft * grad_soft, axis=-1, keepdims=True))
        grad_scores = (score_scale * soft * (grad_soft - delta)).astype(b16).astype(f32)
        grad_queries = jnp.einsum('hqk,khd->qhd', grad_scores, key_rows.astype(f32))
        grad_keys = jnp.einsum('hqk,qhd->khd', grad_scores, queries.astype(f32))
        grad_values = jnp.einsum('hqk,qhd->khd', soft16.astype(f32), grad_att.astype(f32))
        grad_mixed = jnp.stack([grad_queries, grad_keys[TOK_DEV:] + from_next[0], grad_values[TOK_DEV:] + from_next[1]], axis=2)
        bias_sums = lax.optimization_barrier(jnp.sum(grad_mixed, axis=0))
        input_bias_grad = jnp.stack([bias_sums[:, 0], bias_sums[:, 2]], axis=1).reshape(2 * D)
        grad_mixed16 = grad_mixed.reshape(TOK_DEV, 3 * D).astype(b16)
        input_weight_grad = jnp.dot(first_in.T, grad_mixed16, preferred_element_type=f32)
        grad_norm1 = jnp.dot(grad_mixed16, input_weight.T, preferred_element_type=f32)
        back1, first_gain_grad, first_shift_grad = norm_back(grad_norm1, normed1, recip1, first_gain)
        input_grad = grad_hidden + back1
        terms = (first_gain_grad, first_shift_grad, input_weight_grad, input_bias_grad, output_weight_grad, output_bias_grad, second_gain_grad, second_shift_grad, expand_weight_grad, expand_bias_grad, reduce_weight_grad, reduce_bias_grad)
        totals = tuple((total + term for total, term in zip(totals, terms)))
        return (((grad_keys[:TOK_DEV], grad_values[:TOK_DEV]), totals), (block_output, input_grad))
    start_next = (jnp.zeros((TOK_DEV, HEADS, HEAD_DIM), jnp.float32), jnp.zeros((TOK_DEV, HEADS, HEAD_DIM), jnp.float32))
    shapes = [(D,), (D,), (D, 3 * D), (2 * D,), (D, D), (D,), (D,), (D,), (D, FF), (FF,), (FF, D), (D,)]
    start_totals = tuple((jnp.zeros(shape, jnp.float32) for shape in shapes))
    (unused_next, totals), (outputs, input_grads) = lax.scan(step, (start_next, start_totals), jnp.arange(SHARDS, dtype=jnp.int32), reverse=True)
    return (outputs.reshape(TOKENS, D), input_grads.reshape(TOKENS, D), totals[0], totals[1], totals[2], totals[3], totals[4], totals[5], totals[6], totals[7], totals[8], totals[9], totals[10], totals[11])
```

```python
import functools

import jax
import jax.numpy as jnp
from jax import lax
from jax.experimental import pallas as pl
from jax.experimental.pallas import tpu as pltpu
from jax.sharding import PartitionSpec as P

HEAD_DIM = 64


EPSILON = 1e-05
GELU_COEF = 0.7978845608028654
CUBIC = 0.044715


def from_behind(value, axis, steps):
    count = lax.axis_size(axis)
    first, last = (max(0, -steps), min(count, count - steps))
    return lax.ppermute(value, axis, [(source, source + steps) for source in range(first, last)])


def greet(axis, count):
    me = lax.axis_index(axis)
    barrier = pltpu.get_barrier_semaphore()

    def signal(step, carry):
        peer = lax.rem(me + step, count)
        pl.semaphore_signal(
            barrier, inc=1, device_id={axis: peer}, device_id_type=pl.DeviceIdType.MESH
        )
        return carry

    lax.fori_loop(1, count, signal, 0)
    pl.semaphore_wait(barrier, count - 1)
    return me


def scatter_kernel(axis, count, parts, *refs):
    sources, results, landed = (refs[:parts], refs[parts : 2 * parts], refs[2 * parts : 3 * parts])
    send_sem, recv_sem = refs[3 * parts :]
    me = greet(axis, count)

    def copy_of(step, part):
        peer = lax.rem(me + step, count)
        return pltpu.make_async_remote_copy(
            src_ref=sources[part].at[peer],
            dst_ref=landed[part].at[step - 1],
            send_sem=send_sem.at[part, step - 1],
            recv_sem=recv_sem.at[part, step - 1],
            device_id={axis: peer},
            device_id_type=pl.DeviceIdType.MESH,
        )

    def begin(step, carry):
        for part in range(parts):
            copy_of(step, part).start()
        return carry

    def finish(step, carry):
        for part in range(parts):
            copy_of(step, part).wait()
        return carry

    lax.fori_loop(1, count, begin, 0)
    lax.fori_loop(1, count, finish, 0)
    for part in range(parts):
        total = sources[part][me].astype(jnp.float32)
        for step in range(count - 1):
            total = total + landed[part][step].astype(jnp.float32)
        results[part][...] = total


def scatter_sum(values, axis, identity):
    count = values[0].shape[0]
    parts = len(values)
    vmem = pl.BlockSpec(memory_space=pltpu.VMEM)
    return pl.pallas_call(
        functools.partial(scatter_kernel, axis, count, parts),
        out_shape=[jax.ShapeDtypeStruct(value.shape[1:], jnp.float32) for value in values],
        in_specs=[vmem] * parts,
        out_specs=[vmem] * parts,
        scratch_shapes=[pltpu.VMEM((count - 1,) + value.shape[1:], value.dtype) for value in values]
        + [pltpu.SemaphoreType.DMA((parts, count - 1)), pltpu.SemaphoreType.DMA((parts, count - 1))],
        compiler_params=pltpu.CompilerParams(
            collective_id=identity, has_side_effects=True, vmem_limit_bytes=40 * 1024 * 1024
        ),
    )(*values)


def gather_kernel(axis, count, source, result, send_sem, recv_sem):
    me = greet(axis, count)

    def copy_of(step):
        return pltpu.make_async_remote_copy(
            src_ref=source,
            dst_ref=result.at[me],
            send_sem=send_sem.at[step - 1],
            recv_sem=recv_sem.at[step - 1],
            device_id={axis: lax.rem(me + step, count)},
            device_id_type=pl.DeviceIdType.MESH,
        )

    def begin(step, carry):
        copy_of(step).start()
        return carry

    def finish(step, carry):
        copy_of(step).wait()
        return carry

    lax.fori_loop(1, count, begin, 0)
    result[me] = source[...]
    lax.fori_loop(1, count, finish, 0)


def gather(value, axis, count, identity):
    vmem = pl.BlockSpec(memory_space=pltpu.VMEM)
    return pl.pallas_call(
        functools.partial(gather_kernel, axis, count),
        out_shape=jax.ShapeDtypeStruct((count,) + value.shape, value.dtype),
        in_specs=[vmem],
        out_specs=vmem,
        scratch_shapes=[
            pltpu.SemaphoreType.DMA((count - 1,)),
            pltpu.SemaphoreType.DMA((count - 1,)),
        ],
        compiler_params=pltpu.CompilerParams(
            collective_id=identity, has_side_effects=True, vmem_limit_bytes=40 * 1024 * 1024
        ),
    )(value)


def layer_norm(values_in, gain_row, shift_row):
    centred = values_in - jnp.mean(values_in, axis=-1, keepdims=True)
    reciprocal = lax.rsqrt(jnp.mean(centred * centred, axis=-1, keepdims=True) + EPSILON)
    normed = centred * reciprocal
    return (normed * gain_row + shift_row, normed, reciprocal)


def norm_back(grad_in, normed, reciprocal, gain_row):
    scaled = grad_in * gain_row
    spread = (
        scaled
        - jnp.mean(scaled, axis=-1, keepdims=True)
        - normed * jnp.mean(scaled * normed, axis=-1, keepdims=True)
    )
    return (reciprocal * spread, jnp.sum(grad_in * normed, axis=0), jnp.sum(grad_in, axis=0))


def gelu_parts(pre_act):
    tanh_value = jnp.tanh(GELU_COEF * (pre_act + CUBIC * pre_act * pre_act * pre_act))
    result = 0.5 * pre_act * (1.0 + tanh_value)
    slope_value = 0.5 * (1.0 + tanh_value) + 0.5 * pre_act * (
        1.0 - tanh_value * tanh_value
    ) * GELU_COEF * (1.0 + 3.0 * CUBIC * pre_act * pre_act)
    return (result, slope_value)


def full_bias(pairs, group_heads):
    shaped = pairs.reshape(group_heads, 2, HEAD_DIM)
    return jnp.stack([shaped[:, 0], jnp.zeros_like(shaped[:, 0]), shaped[:, 1]], axis=1).reshape(
        group_heads * 3 * HEAD_DIM
    )


def masked_scores(queries, key_rows, allowed):
    scores = jnp.einsum(
        "qhd,khd->hqk", queries, key_rows, preferred_element_type=jnp.float32
    ) * HEAD_DIM ** (-0.5)
    return jnp.where(allowed[None], scores, -1e30)


def per_device(
    block_input,
    first_gain,
    first_shift,
    input_weight,
    input_bias,
    output_weight,
    output_bias,
    second_gain,
    second_shift,
    expand_weight,
    expand_bias,
    reduce_weight,
    reduce_bias,
    output_grad,
    segment_ids,
    shard_counts,
):
    f32 = jnp.float32
    b16 = jnp.bfloat16
    block_rows = block_input.shape[0]
    group_heads = output_weight.shape[0] // HEAD_DIM
    group_width = group_heads * HEAD_DIM
    score_scale = HEAD_DIM ** (-0.5)
    tensor_count = lax.axis_size("tensor")
    share_rows = block_rows // tensor_count
    row_start = lax.axis_index("tensor") * share_rows

    def own_rows(values):
        return lax.dynamic_slice_in_dim(values, row_start, share_rows, 0)

    shard_index = lax.axis_index("dp")
    prior_index = jnp.maximum(shard_index - 1, 0)
    position = jnp.arange(block_rows, dtype=jnp.int32)
    own_ids = lax.dynamic_slice_in_dim(segment_ids, shard_index * block_rows, block_rows)
    prior_ids = lax.dynamic_slice_in_dim(segment_ids, prior_index * block_rows, block_rows)
    own_live = position < shard_counts[shard_index]
    prior_live = (position < shard_counts[prior_index]) & (shard_index > 0)
    diagonal = position[None, :] == position[:, None]
    same_own = (
        (own_ids[:, None] == own_ids[None, :])
        & (position[None, :] <= position[:, None])
        & (own_live[None, :] | diagonal)
    )
    same_prior = (own_ids[:, None] == prior_ids[None, :]) & prior_live[None, :]
    allowed = jnp.concatenate([same_prior, same_own], axis=1)
    live_col = own_live.astype(f32)[:, None]
    first_out, normed1, recip1 = layer_norm(block_input, first_gain, first_shift)
    first_in = first_out.astype(b16)
    mixed = jnp.dot(first_in, input_weight, preferred_element_type=f32) + full_bias(
        input_bias, group_heads
    )
    mixed = mixed.astype(b16).reshape(block_rows, group_heads, 3, HEAD_DIM)
    queries = mixed[:, :, 0]
    own_pair = jnp.concatenate([mixed[:, :, 1], mixed[:, :, 2]], axis=1).reshape(
        block_rows, 2 * group_width
    )
    prior_pair = from_behind(own_pair, "dp", 1).reshape(block_rows, 2 * group_heads, HEAD_DIM)
    key_rows = jnp.concatenate([prior_pair[:, :group_heads], mixed[:, :, 1]], axis=0)
    value_rows = jnp.concatenate([prior_pair[:, group_heads:], mixed[:, :, 2]], axis=0)
    scores = masked_scores(queries, key_rows, allowed)
    row_top = jnp.max(scores, axis=-1, keepdims=True)
    logsum = row_top + jnp.log(jnp.sum(jnp.exp(scores - row_top), axis=-1, keepdims=True))
    soft16 = jnp.exp(scores - logsum).astype(b16)
    attended = (
        jnp.einsum("hqk,khd->qhd", soft16, value_rows, preferred_element_type=f32)
        .astype(b16)
        .reshape(block_rows, group_width)
    )
    in_shares = (tensor_count, share_rows, block_input.shape[1])
    (mixed_rows,) = scatter_sum(
        [jnp.dot(attended, output_weight, preferred_element_type=f32).astype(b16).reshape(in_shares)],
        "tensor",
        0,
    )
    hidden_rows = own_rows(block_input) + mixed_rows + output_bias
    second_out, normed2, recip2 = layer_norm(hidden_rows, second_gain, second_shift)
    second_in = gather(second_out.astype(b16), "tensor", tensor_count, 1).reshape(block_input.shape)
    pre_act = jnp.dot(second_in, expand_weight, preferred_element_type=f32) + expand_bias
    activ, gelu_slope = gelu_parts(pre_act)
    activated = activ.astype(b16)
    feed_part = jnp.dot(activated, reduce_weight, preferred_element_type=f32)
    grad_y = live_col * output_grad
    grad_y16 = grad_y.astype(b16)
    grad_pre = (
        jnp.einsum("rd,kd->rk", grad_y16, reduce_weight, preferred_element_type=f32) * gelu_slope
    )
    grad_pre16 = grad_pre.astype(b16)
    expand_bias_grad = jnp.sum(grad_pre, axis=0)
    norm2_part = jnp.einsum("rk,dk->rd", grad_pre16, expand_weight, preferred_element_type=f32)
    feed_rows, grad_norm2 = scatter_sum(
        [feed_part.astype(b16).reshape(in_shares), norm2_part.astype(b16).reshape(in_shares)],
        "tensor",
        2,
    )
    block_output = own_rows(live_col) * (hidden_rows + feed_rows + reduce_bias)
    back2, second_gain_part, second_shift_part = norm_back(grad_norm2, normed2, recip2, second_gain)
    grad_rows = own_rows(grad_y) + back2
    grad_hidden16 = gather(grad_rows.astype(b16), "tensor", tensor_count, 3).reshape(
        block_input.shape
    )
    output_weight_grad = jnp.einsum(
        "rd,rk->dk", grad_hidden16, attended, preferred_element_type=f32
    )
    grad_att = (
        jnp.einsum("rd,kd->rk", grad_hidden16, output_weight, preferred_element_type=f32)
        .astype(b16)
        .reshape(block_rows, group_heads, HEAD_DIM)
    )
    scores = masked_scores(queries, key_rows, allowed)
    soft = jnp.exp(scores - logsum)
    grad_soft = jnp.einsum("qhd,khd->hqk", grad_att, value_rows, preferred_element_type=f32)
    delta = jnp.sum(soft * grad_soft, axis=-1, keepdims=True)
    grad_scores = (score_scale * soft * (grad_soft - delta)).astype(b16)
    grad_queries = jnp.einsum("hqk,khd->qhd", grad_scores, key_rows, preferred_element_type=f32)
    grad_keys = jnp.einsum("hqk,qhd->khd", grad_scores, queries, preferred_element_type=f32)
    grad_values = jnp.einsum("hqk,qhd->khd", soft.astype(b16), grad_att, preferred_element_type=f32)
    back_pair = jnp.concatenate([grad_keys[:block_rows], grad_values[:block_rows]], axis=1).reshape(
        block_rows, 2 * group_width
    )
    from_next = from_behind(back_pair.astype(b16), "dp", -1).reshape(
        block_rows, 2 * group_heads, HEAD_DIM
    )
    grad_mixed = jnp.stack(
        [
            grad_queries,
            grad_keys[block_rows:] + from_next[:, :group_heads],
            grad_values[block_rows:] + from_next[:, group_heads:],
        ],
        axis=2,
    )
    bias_sums = jnp.sum(grad_mixed, axis=0)
    input_bias_grad = jnp.stack([bias_sums[:, 0], bias_sums[:, 2]], axis=1).reshape(2 * group_width)
    grad_mixed16 = grad_mixed.reshape(block_rows, 3 * group_width).astype(b16)
    norm1_part = jnp.einsum("rc,dc->rd", grad_mixed16, input_weight, preferred_element_type=f32)
    (grad_norm1,) = scatter_sum([norm1_part.astype(b16).reshape(in_shares)], "tensor", 4)
    back1, first_gain_part, first_shift_part = norm_back(
        grad_norm1, own_rows(normed1), own_rows(recip1), first_gain
    )
    input_grad = grad_rows + back1
    input_weight_grad = jnp.einsum("rd,rc->dc", first_in, grad_mixed16, preferred_element_type=f32)
    expand_weight_grad = jnp.einsum("rd,rk->dk", second_in, grad_pre16, preferred_element_type=f32)
    reduce_weight_grad = jnp.einsum("rd,rk->dk", grad_y16, activated, preferred_element_type=f32)
    shard_count = lax.axis_size("dp")

    def pieces(value):
        return value.reshape(shard_count, value.shape[0] // shard_count, value.shape[1])

    wide = expand_bias_grad.shape[0] // shard_count
    narrow = input_bias_grad.shape[0] // shard_count
    vectors = jnp.stack(
        [
            value.reshape(shard_count, -1)
            for value in (
                first_gain_part,
                first_shift_part,
                jnp.sum(grad_rows, axis=0),
                second_gain_part,
                second_shift_part,
                jnp.sum(own_rows(grad_y), axis=0),
            )
        ],
        axis=1,
    )
    biases = jnp.stack(
        [
            expand_bias_grad.reshape(shard_count, wide),
            jnp.pad(input_bias_grad.reshape(shard_count, narrow), ((0, 0), (0, wide - narrow))),
        ],
        axis=1,
    )
    input_sum, output_sum, expand_sum, reduce_sum, vector_sum, bias_sum = scatter_sum(
        [
            pieces(input_weight_grad.astype(b16)),
            pieces(output_weight_grad.astype(b16)),
            pieces(expand_weight_grad.astype(b16)),
            pieces(reduce_weight_grad.astype(b16)),
            vectors,
            biases,
        ],
        "dp",
        5,
    )
    vector_total = jnp.sum(gather(vector_sum, "tensor", tensor_count, 6), axis=0)
    return (
        block_output,
        input_grad,
        vector_total[0],
        vector_total[1],
        input_sum,
        bias_sum[1, :narrow],
        output_sum.T,
        vector_total[2],
        vector_total[3],
        vector_total[4],
        expand_sum,
        bias_sum[0],
        reduce_sum.T,
        vector_total[5],
    )


def solution(mesh):
    placed = (
        P("dp", None),
        P(),
        P(),
        P(None, "tensor"),
        P("tensor"),
        P("tensor", None),
        P(),
        P(),
        P(),
        P(None, "tensor"),
        P("tensor"),
        P("tensor", None),
        P(),
        P("dp", None),
        P(),
        P(),
    )
    return jax.shard_map(
        per_device,
        mesh=mesh,
        in_specs=placed,
        out_specs=(
            P(("dp", "tensor"), None),
            P(("dp", "tensor"), None),
            P("dp"),
            P("dp"),
            P("dp", "tensor"),
            P(("tensor", "dp")),
            P("tensor", "dp"),
            P("dp"),
            P("dp"),
            P("dp"),
            P("dp", "tensor"),
            P(("tensor", "dp")),
            P("tensor", "dp"),
            P("dp"),
        ),
        check_vma=False,
    )
```

```python
import functools

import jax
import jax.numpy as jnp
from jax import lax
from jax.experimental import pallas as pl
from jax.experimental.pallas import tpu as pltpu
from jax.sharding import PartitionSpec as P

HEAD_DIM = 64


EPSILON = 1e-05
GELU_COEF = 0.7978845608028654
CUBIC = 0.044715


def from_behind(value, axis, steps):
    count = lax.axis_size(axis)
    first, last = (max(0, -steps), min(count, count - steps))
    return lax.ppermute(value, axis, [(source, source + steps) for source in range(first, last)])


def greet(axis, count):
    me = lax.axis_index(axis)
    barrier = pltpu.get_barrier_semaphore()

    def signal(step, carry):
        peer = lax.rem(me + step, count)
        pl.semaphore_signal(
            barrier, inc=1, device_id={axis: peer}, device_id_type=pl.DeviceIdType.MESH
        )
        return carry

    lax.fori_loop(1, count, signal, 0)
    pl.semaphore_wait(barrier, count - 1)
    return me


def scatter_kernel(axis, count, parts, *refs):
    sources, results, landed = (refs[:parts], refs[parts : 2 * parts], refs[2 * parts : 3 * parts])
    send_sem, recv_sem = refs[3 * parts :]
    me = greet(axis, count)

    def copy_of(step, part):
        peer = lax.rem(me + step, count)
        return pltpu.make_async_remote_copy(
            src_ref=sources[part].at[peer],
            dst_ref=landed[part].at[step - 1],
            send_sem=send_sem.at[part, step - 1],
            recv_sem=recv_sem.at[part, step - 1],
            device_id={axis: peer},
            device_id_type=pl.DeviceIdType.MESH,
        )

    def begin(step, carry):
        for part in range(parts):
            copy_of(step, part).start()
        return carry

    def finish(step, carry):
        for part in range(parts):
            copy_of(step, part).wait()
        return carry

    lax.fori_loop(1, count, begin, 0)
    lax.fori_loop(1, count, finish, 0)
    for part in range(parts):
        total = sources[part][me].astype(jnp.float32)
        for step in range(count - 1):
            total = total + landed[part][step].astype(jnp.float32)
        results[part][...] = total


def scatter_sum(values, axis, identity):
    count = values[0].shape[0]
    parts = len(values)
    vmem = pl.BlockSpec(memory_space=pltpu.VMEM)
    return pl.pallas_call(
        functools.partial(scatter_kernel, axis, count, parts),
        out_shape=[jax.ShapeDtypeStruct(value.shape[1:], jnp.float32) for value in values],
        in_specs=[vmem] * parts,
        out_specs=[vmem] * parts,
        scratch_shapes=[pltpu.VMEM((count - 1,) + value.shape[1:], value.dtype) for value in values]
        + [pltpu.SemaphoreType.DMA((parts, count - 1)), pltpu.SemaphoreType.DMA((parts, count - 1))],
        compiler_params=pltpu.CompilerParams(
            collective_id=identity, has_side_effects=True, vmem_limit_bytes=40 * 1024 * 1024
        ),
    )(*values)


def gather_kernel(axis, count, source, result, send_sem, recv_sem):
    me = greet(axis, count)

    def copy_of(step):
        return pltpu.make_async_remote_copy(
            src_ref=source,
            dst_ref=result.at[me],
            send_sem=send_sem.at[step - 1],
            recv_sem=recv_sem.at[step - 1],
            device_id={axis: lax.rem(me + step, count)},
            device_id_type=pl.DeviceIdType.MESH,
        )

    def begin(step, carry):
        copy_of(step).start()
        return carry

    def finish(step, carry):
        copy_of(step).wait()
        return carry

    lax.fori_loop(1, count, begin, 0)
    result[me] = source[...]
    lax.fori_loop(1, count, finish, 0)


def gather(value, axis, count, identity):
    vmem = pl.BlockSpec(memory_space=pltpu.VMEM)
    return pl.pallas_call(
        functools.partial(gather_kernel, axis, count),
        out_shape=jax.ShapeDtypeStruct((count,) + value.shape, value.dtype),
        in_specs=[vmem],
        out_specs=vmem,
        scratch_shapes=[
            pltpu.SemaphoreType.DMA((count - 1,)),
            pltpu.SemaphoreType.DMA((count - 1,)),
        ],
        compiler_params=pltpu.CompilerParams(
            collective_id=identity, has_side_effects=True, vmem_limit_bytes=40 * 1024 * 1024
        ),
    )(value)


def across(left, right, left_dim, right_dim):
    return lax.dot_general(
        left, right, (((left_dim,), (right_dim,)), ((), ())), preferred_element_type=jnp.float32
    )


def norm_back_rows(grad_in, normed, reciprocal, gain_row):
    scaled = grad_in * gain_row
    spread = (
        scaled
        - jnp.mean(scaled, axis=-1, keepdims=True)
        - normed * jnp.mean(scaled * normed, axis=-1, keepdims=True)
    )
    return (
        reciprocal * spread,
        jnp.sum(grad_in * normed, axis=0, keepdims=True),
        jnp.sum(grad_in, axis=0, keepdims=True),
    )


def tail_kernel(
    shards,
    groups,
    heads,
    feed_ref,
    norm2_ref,
    expand_ref,
    reduce_ref,
    hidden_ref,
    normed2_ref,
    recip2_ref,
    gain2_ref,
    reduce_bias_ref,
    grad_y_ref,
    live_ref,
    expand_bias_ref,
    attended_ref,
    output_weight_ref,
    query_ref,
    key_ref,
    value_ref,
    soft_ref,
    first_in_ref,
    input_weight_ref,
    normed1_ref,
    recip1_ref,
    gain1_ref,
    block_out,
    input_out,
    input_sum,
    output_sum,
    expand_sum,
    reduce_sum,
    vector_sum,
    norm2_land,
    feed_land,
    rows16,
    rows_all,
    norm1_part,
    norm1_land,
    vector_part,
    vector_land,
    vector_own,
    vector_far,
    back_own,
    back_land,
    mixed_grad,
    output_part,
    input_part,
    expand_land,
    reduce_land,
    output_land,
    input_land,
    tensor_send,
    tensor_recv,
    dp_send,
    dp_recv,
    back_send,
    back_recv,
):
    f32 = jnp.float32
    b16 = jnp.bfloat16
    mesh_id = pl.DeviceIdType.MESH
    my_shard = lax.axis_index("dp")
    my_group = lax.axis_index("tensor")
    barrier = pltpu.get_barrier_semaphore()

    def signal_dp(step, carry):
        pl.semaphore_signal(
            barrier, inc=1, device_id={"dp": lax.rem(my_shard + step, shards)}, device_id_type=mesh_id
        )
        return carry

    def signal_tensor(step, carry):
        pl.semaphore_signal(
            barrier,
            inc=1,
            device_id={"tensor": lax.rem(my_group + step, groups)},
            device_id_type=mesh_id,
        )
        return carry

    lax.fori_loop(1, groups, signal_tensor, 0)
    lax.fori_loop(1, shards, signal_dp, 0)
    pl.semaphore_wait(barrier, shards + groups - 2)

    def tensor_copy(kind, source, target, step):
        peer = lax.rem(my_group + step, groups)
        return pltpu.make_async_remote_copy(
            src_ref=source(peer),
            dst_ref=target(step),
            send_sem=tensor_send.at[kind, step - 1],
            recv_sem=tensor_recv.at[kind, step - 1],
            device_id={"tensor": peer},
            device_id_type=mesh_id,
        )

    def dp_copy(kind, source, target, step):
        peer = lax.rem(my_shard + step, shards)
        return pltpu.make_async_remote_copy(
            src_ref=source(peer),
            dst_ref=target.at[step - 1],
            send_sem=dp_send.at[kind, step - 1],
            recv_sem=dp_recv.at[kind, step - 1],
            device_id={"dp": peer},
            device_id_type=mesh_id,
        )

    def begin(copy, kind, source, target, count):
        def run(step, carry):
            copy(kind, source, target, step).start()
            return carry

        lax.fori_loop(1, count, run, 0)

    def finish(copy, kind, source, target, count):
        def run(step, carry):
            copy(kind, source, target, step).wait()
            return carry

        lax.fori_loop(1, count, run, 0)

    norm2_move = (tensor_copy, 0, lambda p: norm2_ref.at[p], lambda t: norm2_land.at[t - 1], groups)
    feed_move = (tensor_copy, 1, lambda p: feed_ref.at[p], lambda t: feed_land.at[t - 1], groups)
    rows_move = (tensor_copy, 2, lambda p: rows16, lambda t: rows_all.at[my_group], groups)
    norm1_move = (tensor_copy, 3, lambda p: norm1_part.at[p], lambda t: norm1_land.at[t - 1], groups)
    vector_move = (tensor_copy, 4, lambda p: vector_part, lambda t: vector_land.at[t - 1], groups)
    reduce_move = (dp_copy, 0, lambda p: reduce_ref.at[p], reduce_land, shards)
    expand_move = (dp_copy, 1, lambda p: expand_ref.at[p], expand_land, shards)
    output_move = (dp_copy, 2, lambda p: output_part.at[p], output_land, shards)
    input_move = (dp_copy, 3, lambda p: input_part.at[p], input_land, shards)
    far_move = (dp_copy, 4, lambda p: vector_own, vector_far, shards)

    def total_of(own, land, count):
        total = own.astype(f32)
        for step in range(count - 1):
            total = total + land[step].astype(f32)
        return total

    begin(*norm2_move)
    begin(*reduce_move)
    begin(*feed_move)
    vector_part[...] = jnp.zeros_like(vector_part)
    finish(*norm2_move)
    grad_norm2 = total_of(norm2_ref[my_group], norm2_land, groups)
    back2, gain_row, shift_row = norm_back_rows(
        grad_norm2, normed2_ref[...], recip2_ref[...], gain2_ref[...]
    )
    grad_y = grad_y_ref[...]
    grad_rows = grad_y + back2
    rows16[...] = grad_rows.astype(b16)
    begin(*rows_move)
    input_out[...] = grad_rows
    rows_all[my_group] = grad_rows.astype(b16)
    width = grad_y.shape[1]
    vector_part[2:3, :width] = jnp.sum(grad_rows, axis=0, keepdims=True)
    vector_part[3:4, :width] = gain_row
    vector_part[4:5, :width] = shift_row
    vector_part[5:6, :width] = jnp.sum(grad_y, axis=0, keepdims=True)
    vector_part[6:7, : expand_bias_ref.shape[1]] = expand_bias_ref[...]
    finish(*feed_move)
    feed_rows = total_of(feed_ref[my_group], feed_land, groups)
    block_out[...] = live_ref[...] * (hidden_ref[...] + feed_rows + reduce_bias_ref[...])
    finish(*rows_move)
    share = rows_all.shape[1]
    rows = groups * share
    hidden16 = rows_all[...].reshape(rows, width)
    grad_att = across(hidden16, output_weight_ref[...], 1, 1).astype(b16)
    scale = HEAD_DIM ** (-0.5)
    span = heads * HEAD_DIM
    for head in range(heads):
        low = head * HEAD_DIM
        high = low + HEAD_DIM
        first = 3 * low
        att = grad_att[:, low:high]
        keys = key_ref[:, low:high]
        soft = soft_ref[head]
        grad_soft = across(att, value_ref[:, low:high], 1, 1)
        delta = jnp.sum(soft * grad_soft, axis=-1, keepdims=True)
        grad_scores = (scale * soft * (grad_soft - delta)).astype(b16)
        grad_keys = across(grad_scores, query_ref[:, low:high], 0, 0)
        grad_values = across(soft.astype(b16), att, 0, 0)
        back_own[:, low:high] = grad_keys[:rows].astype(b16)
        back_own[:, span + low : span + high] = grad_values[:rows].astype(b16)
        mixed_grad[:, first : first + HEAD_DIM] = across(grad_scores, keys, 1, 0)
        mixed_grad[:, first + HEAD_DIM : first + 2 * HEAD_DIM] = grad_keys[rows:]
        mixed_grad[:, first + 2 * HEAD_DIM : first + 3 * HEAD_DIM] = grad_values[rows:]

    back_copy = pltpu.make_async_remote_copy(
        src_ref=back_own,
        dst_ref=back_land,
        send_sem=back_send,
        recv_sem=back_recv,
        device_id={"dp": lax.rem(my_shard + shards - 1, shards)},
        device_id_type=mesh_id,
    )

    @pl.when(my_shard > 0)
    def _():
        back_copy.start()

    begin(*expand_move)
    output_grad = across(hidden16, attended_ref[...], 0, 0)
    piece = output_part.shape[1]
    for part in range(shards):
        output_part[part] = output_grad[part * piece : (part + 1) * piece].astype(b16)
    begin(*output_move)

    @pl.when(my_shard < shards - 1)
    def _():
        back_copy.wait_recv()

    @pl.when(my_shard == shards - 1)
    def _():
        back_land[...] = jnp.zeros_like(back_land)

    for head in range(heads):
        low = head * HEAD_DIM
        high = low + HEAD_DIM
        key_at = 3 * low + HEAD_DIM
        value_at = key_at + HEAD_DIM
        mixed_grad[:, key_at:value_at] += back_land[:, low:high].astype(f32)
        mixed_grad[:, value_at : value_at + HEAD_DIM] += back_land[
            :, span + low : span + high
        ].astype(f32)
    mixed = mixed_grad[...]
    mixed16 = mixed.astype(b16)
    norm1 = across(mixed16, input_weight_ref[...], 1, 1).astype(b16)
    norm1_part[...] = norm1.reshape(groups, share, width)
    begin(*norm1_move)
    input_grad = across(first_in_ref[...], mixed16, 0, 0)
    for part in range(shards):
        input_part[part] = input_grad[part * piece : (part + 1) * piece].astype(b16)
    begin(*input_move)
    vector_part[7:8, : mixed.shape[1]] = jnp.sum(mixed, axis=0, keepdims=True)
    finish(*norm1_move)
    grad_norm1 = total_of(norm1_part[my_group], norm1_land, groups)
    back1, gain_row, shift_row = norm_back_rows(
        grad_norm1, normed1_ref[...], recip1_ref[...], gain1_ref[...]
    )
    vector_part[0:1, :width] = gain_row
    vector_part[1:2, :width] = shift_row
    begin(*vector_move)
    input_out[...] += back1
    finish(*vector_move)
    own = vector_part[...]
    added = vector_land[0]
    for step in range(1, groups - 1):
        added = added + vector_land[step]
    row_index = lax.broadcasted_iota(jnp.int32, own.shape, 0)
    vector_own[...] = own + jnp.where(row_index < 6, added, 0.0)
    begin(*far_move)

    @pl.when(my_shard > 0)
    def _():
        back_copy.wait_send()

    finish(*reduce_move)
    reduce_sum[...] = total_of(reduce_ref[my_shard], reduce_land, shards)
    finish(*expand_move)
    expand_sum[...] = total_of(expand_ref[my_shard], expand_land, shards)
    finish(*output_move)
    output_sum[...] = total_of(output_part[my_shard], output_land, shards)
    finish(*input_move)
    input_sum[...] = total_of(input_part[my_shard], input_land, shards)
    finish(*far_move)
    vector_sum[...] = total_of(vector_own[...], vector_far, shards)


def tail(shards, groups, heads, operands):
    f32 = jnp.float32
    b16 = jnp.bfloat16
    share, width = operands[4].shape
    rows = share * groups
    piece = operands[2].shape[1]
    hidden = operands[2].shape[2]
    span = heads * HEAD_DIM
    broad = max(width, hidden, 3 * span)
    vmem = pl.BlockSpec(memory_space=pltpu.VMEM)

    def shape(*sizes):
        return jax.ShapeDtypeStruct(sizes, f32)

    dma = pltpu.SemaphoreType.DMA
    return pl.pallas_call(
        functools.partial(tail_kernel, shards, groups, heads),
        out_shape=[
            shape(share, width),
            shape(share, width),
            shape(piece, 3 * span),
            shape(piece, span),
            shape(piece, hidden),
            shape(piece, hidden),
            shape(8, broad),
        ],
        in_specs=[vmem] * len(operands),
        out_specs=[vmem] * 7,
        scratch_shapes=[
            pltpu.VMEM((groups - 1, share, width), b16),
            pltpu.VMEM((groups - 1, share, width), b16),
            pltpu.VMEM((share, width), b16),
            pltpu.VMEM((groups, share, width), b16),
            pltpu.VMEM((groups, share, width), b16),
            pltpu.VMEM((groups - 1, share, width), b16),
            pltpu.VMEM((8, broad), f32),
            pltpu.VMEM((groups - 1, 8, broad), f32),
            pltpu.VMEM((8, broad), f32),
            pltpu.VMEM((shards - 1, 8, broad), f32),
            pltpu.VMEM((rows, 2 * span), b16),
            pltpu.VMEM((rows, 2 * span), b16),
            pltpu.VMEM((rows, 3 * span), f32),
            pltpu.VMEM((shards, piece, span), b16),
            pltpu.VMEM((shards, piece, 3 * span), b16),
            pltpu.VMEM((shards - 1, piece, hidden), b16),
            pltpu.VMEM((shards - 1, piece, hidden), b16),
            pltpu.VMEM((shards - 1, piece, span), b16),
            pltpu.VMEM((shards - 1, piece, 3 * span), b16),
            dma((5, groups - 1)),
            dma((5, groups - 1)),
            dma((5, shards - 1)),
            dma((5, shards - 1)),
            dma,
            dma,
        ],
        compiler_params=pltpu.CompilerParams(
            collective_id=2, has_side_effects=True, vmem_limit_bytes=48 * 1024 * 1024
        ),
    )(*operands)


def layer_norm(values_in, gain_row, shift_row):
    centred = values_in - jnp.mean(values_in, axis=-1, keepdims=True)
    reciprocal = lax.rsqrt(jnp.mean(centred * centred, axis=-1, keepdims=True) + EPSILON)
    normed = centred * reciprocal
    return (normed * gain_row + shift_row, normed, reciprocal)


def gelu_parts(pre_act):
    tanh_value = jnp.tanh(GELU_COEF * (pre_act + CUBIC * pre_act * pre_act * pre_act))
    result = 0.5 * pre_act * (1.0 + tanh_value)
    slope_value = 0.5 * (1.0 + tanh_value) + 0.5 * pre_act * (
        1.0 - tanh_value * tanh_value
    ) * GELU_COEF * (1.0 + 3.0 * CUBIC * pre_act * pre_act)
    return (result, slope_value)


def full_bias(pairs, group_heads):
    shaped = pairs.reshape(group_heads, 2, HEAD_DIM)
    return jnp.stack([shaped[:, 0], jnp.zeros_like(shaped[:, 0]), shaped[:, 1]], axis=1).reshape(
        group_heads * 3 * HEAD_DIM
    )


def masked_scores(queries, key_rows, allowed):
    scores = jnp.einsum(
        "qhd,khd->hqk", queries, key_rows, preferred_element_type=jnp.float32
    ) * HEAD_DIM ** (-0.5)
    return jnp.where(allowed[None], scores, -1e30)


def per_device(
    block_input,
    first_gain,
    first_shift,
    input_weight,
    input_bias,
    output_weight,
    output_bias,
    second_gain,
    second_shift,
    expand_weight,
    expand_bias,
    reduce_weight,
    reduce_bias,
    output_grad,
    segment_ids,
    shard_counts,
):
    f32 = jnp.float32
    b16 = jnp.bfloat16
    block_rows = block_input.shape[0]
    group_heads = output_weight.shape[0] // HEAD_DIM
    group_width = group_heads * HEAD_DIM
    score_scale = HEAD_DIM ** (-0.5)
    tensor_count = lax.axis_size("tensor")
    share_rows = block_rows // tensor_count
    row_start = lax.axis_index("tensor") * share_rows

    def own_rows(values):
        return lax.dynamic_slice_in_dim(values, row_start, share_rows, 0)

    shard_index = lax.axis_index("dp")
    prior_index = jnp.maximum(shard_index - 1, 0)
    position = jnp.arange(block_rows, dtype=jnp.int32)
    own_ids = lax.dynamic_slice_in_dim(segment_ids, shard_index * block_rows, block_rows)
    prior_ids = lax.dynamic_slice_in_dim(segment_ids, prior_index * block_rows, block_rows)
    own_live = position < shard_counts[shard_index]
    prior_live = (position < shard_counts[prior_index]) & (shard_index > 0)
    diagonal = position[None, :] == position[:, None]
    same_own = (
        (own_ids[:, None] == own_ids[None, :])
        & (position[None, :] <= position[:, None])
        & (own_live[None, :] | diagonal)
    )
    same_prior = (own_ids[:, None] == prior_ids[None, :]) & prior_live[None, :]
    allowed = jnp.concatenate([same_prior, same_own], axis=1)
    live_col = own_live.astype(f32)[:, None]
    first_out, normed1, recip1 = layer_norm(block_input, first_gain, first_shift)
    first_in = first_out.astype(b16)
    mixed = jnp.dot(first_in, input_weight, preferred_element_type=f32) + full_bias(
        input_bias, group_heads
    )
    mixed = mixed.astype(b16).reshape(block_rows, group_heads, 3, HEAD_DIM)
    queries = mixed[:, :, 0]
    own_pair = jnp.concatenate([mixed[:, :, 1], mixed[:, :, 2]], axis=1).reshape(
        block_rows, 2 * group_width
    )
    prior_pair = from_behind(own_pair, "dp", 1).reshape(block_rows, 2 * group_heads, HEAD_DIM)
    key_rows = jnp.concatenate([prior_pair[:, :group_heads], mixed[:, :, 1]], axis=0)
    value_rows = jnp.concatenate([prior_pair[:, group_heads:], mixed[:, :, 2]], axis=0)
    scores = masked_scores(queries, key_rows, allowed)
    row_top = jnp.max(scores, axis=-1, keepdims=True)
    logsum = row_top + jnp.log(jnp.sum(jnp.exp(scores - row_top), axis=-1, keepdims=True))
    soft = jnp.exp(scores - logsum)
    soft16 = soft.astype(b16)
    attended = (
        jnp.einsum("hqk,khd->qhd", soft16, value_rows, preferred_element_type=f32)
        .astype(b16)
        .reshape(block_rows, group_width)
    )
    in_shares = (tensor_count, share_rows, block_input.shape[1])
    (mixed_rows,) = scatter_sum(
        [jnp.dot(attended, output_weight, preferred_element_type=f32).astype(b16).reshape(in_shares)],
        "tensor",
        0,
    )
    hidden_rows = own_rows(block_input) + mixed_rows + output_bias
    second_out, normed2, recip2 = layer_norm(hidden_rows, second_gain, second_shift)
    second_in = gather(second_out.astype(b16), "tensor", tensor_count, 1).reshape(block_input.shape)
    pre_act = jnp.dot(second_in, expand_weight, preferred_element_type=f32) + expand_bias
    activ, gelu_slope = gelu_parts(pre_act)
    activated = activ.astype(b16)
    feed_part = jnp.dot(activated, reduce_weight, preferred_element_type=f32)
    grad_y = live_col * output_grad
    grad_y16 = grad_y.astype(b16)
    grad_pre = (
        jnp.einsum("rd,kd->rk", grad_y16, reduce_weight, preferred_element_type=f32) * gelu_slope
    )
    grad_pre16 = grad_pre.astype(b16)
    expand_bias_grad = jnp.sum(grad_pre, axis=0)
    norm2_part = jnp.einsum("rk,dk->rd", grad_pre16, expand_weight, preferred_element_type=f32)
    shard_count = lax.axis_size("dp")
    expand_weight_grad = jnp.einsum("rd,rk->dk", second_in, grad_pre16, preferred_element_type=f32)
    reduce_weight_grad = jnp.einsum("rd,rk->dk", grad_y16, activated, preferred_element_type=f32)

    def pieces(value):
        return value.reshape(shard_count, value.shape[0] // shard_count, value.shape[1])

    def two_rows(values):
        return values.reshape(values.shape[0], group_width)

    block_output, input_grad, input_sum, output_sum, expand_sum, reduce_sum, vectors = tail(
        shard_count,
        tensor_count,
        group_heads,
        [
            feed_part.astype(b16).reshape(in_shares),
            norm2_part.astype(b16).reshape(in_shares),
            pieces(expand_weight_grad.astype(b16)),
            pieces(reduce_weight_grad.astype(b16)),
            hidden_rows,
            normed2,
            recip2,
            second_gain[None],
            reduce_bias[None],
            own_rows(grad_y),
            own_rows(live_col),
            expand_bias_grad[None],
            attended,
            output_weight,
            two_rows(queries),
            two_rows(key_rows),
            two_rows(value_rows),
            soft,
            first_in,
            input_weight,
            own_rows(normed1),
            own_rows(recip1),
            first_gain[None],
        ],
    )
    features = block_input.shape[1]
    bias_pairs = vectors[7, : 3 * group_width].reshape(group_heads, 3, HEAD_DIM)
    input_bias_grad = jnp.stack([bias_pairs[:, 0], bias_pairs[:, 2]], axis=1).reshape(
        2 * group_width
    )

    def own_piece(value):
        size = value.shape[-1] // shard_count
        return lax.dynamic_slice_in_dim(value, shard_index * size, size, value.ndim - 1)

    vector_total = own_piece(vectors[:6, :features])
    return (
        block_output,
        input_grad,
        vector_total[0],
        vector_total[1],
        input_sum,
        own_piece(input_bias_grad),
        output_sum.T,
        vector_total[2],
        vector_total[3],
        vector_total[4],
        expand_sum,
        own_piece(vectors[6, : expand_bias_grad.shape[0]]),
        reduce_sum.T,
        vector_total[5],
    )


def solution(mesh):
    placed = (
        P("dp", None),
        P(),
        P(),
        P(None, "tensor"),
        P("tensor"),
        P("tensor", None),
        P(),
        P(),
        P(),
        P(None, "tensor"),
        P("tensor"),
        P("tensor", None),
        P(),
        P("dp", None),
        P(),
        P(),
    )
    return jax.shard_map(
        per_device,
        mesh=mesh,
        in_specs=placed,
        out_specs=(
            P(("dp", "tensor"), None),
            P(("dp", "tensor"), None),
            P("dp"),
            P("dp"),
            P("dp", "tensor"),
            P(("tensor", "dp")),
            P("tensor", "dp"),
            P("dp"),
            P("dp"),
            P("dp"),
            P("dp", "tensor"),
            P(("tensor", "dp")),
            P("tensor", "dp"),
            P("dp"),
        ),
        check_vma=False,
    )
```

```python
import functools

import jax
import jax.numpy as jnp
from jax import lax
from jax.experimental import pallas as pl
from jax.experimental.pallas import tpu as pltpu
from jax.sharding import PartitionSpec as P

HEAD_DIM = 64


EPSILON = 1e-05
GELU_COEF = 0.7978845608028654
CUBIC = 0.044715


def from_behind(value, axis, steps):
    count = lax.axis_size(axis)
    first, last = (max(0, -steps), min(count, count - steps))
    return lax.ppermute(value, axis, [(source, source + steps) for source in range(first, last)])


def greet(axis, count):
    me = lax.axis_index(axis)
    barrier = pltpu.get_barrier_semaphore()

    def signal(step, carry):
        peer = lax.rem(me + step, count)
        pl.semaphore_signal(
            barrier, inc=1, device_id={axis: peer}, device_id_type=pl.DeviceIdType.MESH
        )
        return carry

    lax.fori_loop(1, count, signal, 0)
    pl.semaphore_wait(barrier, count - 1)
    return me


def scatter_kernel(axis, count, parts, *refs):
    sources, results, landed = (refs[:parts], refs[parts : 2 * parts], refs[2 * parts : 3 * parts])
    send_sem, recv_sem = refs[3 * parts :]
    me = greet(axis, count)

    def copy_of(step, part):
        peer = lax.rem(me + step, count)
        return pltpu.make_async_remote_copy(
            src_ref=sources[part].at[peer],
            dst_ref=landed[part].at[step - 1],
            send_sem=send_sem.at[part, step - 1],
            recv_sem=recv_sem.at[part, step - 1],
            device_id={axis: peer},
            device_id_type=pl.DeviceIdType.MESH,
        )

    def begin(step, carry):
        for part in range(parts):
            copy_of(step, part).start()
        return carry

    def finish(step, carry):
        for part in range(parts):
            copy_of(step, part).wait()
        return carry

    lax.fori_loop(1, count, begin, 0)
    lax.fori_loop(1, count, finish, 0)
    for part in range(parts):
        total = sources[part][me].astype(jnp.float32)
        for step in range(count - 1):
            total = total + landed[part][step].astype(jnp.float32)
        results[part][...] = total


def scatter_sum(values, axis, identity):
    count = values[0].shape[0]
    parts = len(values)
    vmem = pl.BlockSpec(memory_space=pltpu.VMEM)
    return pl.pallas_call(
        functools.partial(scatter_kernel, axis, count, parts),
        out_shape=[jax.ShapeDtypeStruct(value.shape[1:], jnp.float32) for value in values],
        in_specs=[vmem] * parts,
        out_specs=[vmem] * parts,
        scratch_shapes=[pltpu.VMEM((count - 1,) + value.shape[1:], value.dtype) for value in values]
        + [pltpu.SemaphoreType.DMA((parts, count - 1)), pltpu.SemaphoreType.DMA((parts, count - 1))],
        compiler_params=pltpu.CompilerParams(
            collective_id=identity, has_side_effects=True, vmem_limit_bytes=40 * 1024 * 1024
        ),
    )(*values)


def gather_kernel(axis, count, source, result, send_sem, recv_sem):
    me = greet(axis, count)

    def copy_of(step):
        return pltpu.make_async_remote_copy(
            src_ref=source,
            dst_ref=result.at[me],
            send_sem=send_sem.at[step - 1],
            recv_sem=recv_sem.at[step - 1],
            device_id={axis: lax.rem(me + step, count)},
            device_id_type=pl.DeviceIdType.MESH,
        )

    def begin(step, carry):
        copy_of(step).start()
        return carry

    def finish(step, carry):
        copy_of(step).wait()
        return carry

    lax.fori_loop(1, count, begin, 0)
    result[me] = source[...]
    lax.fori_loop(1, count, finish, 0)


def gather(value, axis, count, identity):
    vmem = pl.BlockSpec(memory_space=pltpu.VMEM)
    return pl.pallas_call(
        functools.partial(gather_kernel, axis, count),
        out_shape=jax.ShapeDtypeStruct((count,) + value.shape, value.dtype),
        in_specs=[vmem],
        out_specs=vmem,
        scratch_shapes=[
            pltpu.SemaphoreType.DMA((count - 1,)),
            pltpu.SemaphoreType.DMA((count - 1,)),
        ],
        compiler_params=pltpu.CompilerParams(
            collective_id=identity, has_side_effects=True, vmem_limit_bytes=40 * 1024 * 1024
        ),
    )(value)


def across(left, right, left_dim, right_dim):
    return lax.dot_general(
        left, right, (((left_dim,), (right_dim,)), ((), ())), preferred_element_type=jnp.float32
    )


def norm_back_rows(grad_in, normed, reciprocal, gain_row):
    scaled = grad_in * gain_row
    spread = (
        scaled
        - jnp.mean(scaled, axis=-1, keepdims=True)
        - normed * jnp.mean(scaled * normed, axis=-1, keepdims=True)
    )
    return (
        reciprocal * spread,
        jnp.sum(grad_in * normed, axis=0, keepdims=True),
        jnp.sum(grad_in, axis=0, keepdims=True),
    )


def attention_kernel(heads, mixed_ref, prior_ref, allowed_ref, attended_ref, soft_ref):
    b16 = jnp.bfloat16
    for head in range(heads):
        low = head * HEAD_DIM
        first = 3 * low
        second = first + HEAD_DIM
        third = second + HEAD_DIM
        keys = jnp.concatenate([prior_ref[:, second:third], mixed_ref[:, second:third]], axis=0)
        values = jnp.concatenate(
            [prior_ref[:, third : third + HEAD_DIM], mixed_ref[:, third : third + HEAD_DIM]], axis=0
        )
        scores = across(mixed_ref[:, first:second], keys, 1, 1) * HEAD_DIM ** (-0.5)
        scores = jnp.where(allowed_ref[...] > 0.0, scores, -1e30)
        row_top = jnp.max(scores, axis=-1, keepdims=True)
        logsum = row_top + jnp.log(jnp.sum(jnp.exp(scores - row_top), axis=-1, keepdims=True))
        soft = jnp.exp(scores - logsum)
        soft_ref[head] = soft
        attended_ref[:, low : low + HEAD_DIM] = across(soft.astype(b16), values, 1, 0).astype(b16)


def attention(heads, mixed, prior, allowed):
    vmem = pl.BlockSpec(memory_space=pltpu.VMEM)
    rows = mixed.shape[0]
    return pl.pallas_call(
        functools.partial(attention_kernel, heads),
        out_shape=[
            jax.ShapeDtypeStruct((rows, heads * HEAD_DIM), jnp.bfloat16),
            jax.ShapeDtypeStruct((heads, rows, 2 * rows), jnp.float32),
        ],
        in_specs=[vmem] * 3,
        out_specs=[vmem] * 2,
        compiler_params=pltpu.CompilerParams(vmem_limit_bytes=32 * 1024 * 1024),
    )(mixed, prior, allowed)


def tail_kernel(
    shards,
    groups,
    heads,
    feed_ref,
    norm2_ref,
    expand_ref,
    reduce_ref,
    hidden_ref,
    normed2_ref,
    recip2_ref,
    gain2_ref,
    reduce_bias_ref,
    grad_y_ref,
    live_ref,
    expand_bias_ref,
    attended_ref,
    output_weight_ref,
    mixed_ref,
    prior_ref,
    soft_ref,
    first_in_ref,
    input_weight_ref,
    normed1_ref,
    recip1_ref,
    gain1_ref,
    block_out,
    input_out,
    input_sum,
    output_sum,
    expand_sum,
    reduce_sum,
    vector_sum,
    norm2_land,
    feed_land,
    rows16,
    rows_all,
    norm1_part,
    norm1_land,
    vector_part,
    vector_land,
    vector_own,
    vector_far,
    back_own,
    back_land,
    mixed_grad,
    output_part,
    input_part,
    reduce_mid,
    expand_mid,
    output_mid,
    input_mid,
    reduce_pair,
    expand_pair,
    output_pair,
    input_pair,
    reduce_land,
    expand_land,
    output_land,
    input_land,
    tensor_send,
    tensor_recv,
    pair_send,
    pair_recv,
    line_send,
    line_recv,
    far_send,
    far_recv,
    back_send,
    back_recv,
):
    f32 = jnp.float32
    b16 = jnp.bfloat16
    mesh_id = pl.DeviceIdType.MESH
    my_shard = lax.axis_index("dp")
    my_group = lax.axis_index("tensor")
    barrier = pltpu.get_barrier_semaphore()

    def signal_dp(step, carry):
        pl.semaphore_signal(
            barrier, inc=1, device_id={"dp": lax.rem(my_shard + step, shards)}, device_id_type=mesh_id
        )
        return carry

    def signal_tensor(step, carry):
        pl.semaphore_signal(
            barrier,
            inc=1,
            device_id={"tensor": lax.rem(my_group + step, groups)},
            device_id_type=mesh_id,
        )
        return carry

    lax.fori_loop(1, groups, signal_tensor, 0)
    lax.fori_loop(1, shards, signal_dp, 0)
    pl.semaphore_wait(barrier, shards + groups - 2)

    def tensor_copy(kind, source, target, step):
        peer = lax.rem(my_group + step, groups)
        return pltpu.make_async_remote_copy(
            src_ref=source(peer),
            dst_ref=target(step),
            send_sem=tensor_send.at[kind, step - 1],
            recv_sem=tensor_recv.at[kind, step - 1],
            device_id={"tensor": peer},
            device_id_type=mesh_id,
        )

    def dp_copy(kind, source, target, step):
        peer = lax.rem(my_shard + step, shards)
        return pltpu.make_async_remote_copy(
            src_ref=source(peer),
            dst_ref=target.at[step - 1],
            send_sem=far_send.at[step - 1],
            recv_sem=far_recv.at[step - 1],
            device_id={"dp": peer},
            device_id_type=mesh_id,
        )

    half = shards // 2
    parity = lax.rem(my_shard, 2)
    place = my_shard // 2
    partner = my_shard + 1 - 2 * parity

    def pair_copy(kind, source, target, step):
        return pltpu.make_async_remote_copy(
            src_ref=source.at[2 * step + 1 - parity],
            dst_ref=target.at[step],
            send_sem=pair_send.at[kind, step],
            recv_sem=pair_recv.at[kind, step],
            device_id={"dp": partner},
            device_id_type=mesh_id,
        )

    def line_copy(kind, source, target, step):
        goal = lax.rem(place + step, half)
        return pltpu.make_async_remote_copy(
            src_ref=source.at[goal],
            dst_ref=target.at[step - 1],
            send_sem=line_send.at[kind, step - 1],
            recv_sem=line_recv.at[kind, step - 1],
            device_id={"dp": 2 * goal + parity},
            device_id_type=mesh_id,
        )

    def begin_pair(kind, source, pair):
        def run(step, carry):
            pair_copy(kind, source, pair, step).start()
            return carry

        lax.fori_loop(0, half, run, 0)

    def begin_line(kind, source, pair, mid, land):
        def run(step, carry):
            pair_copy(kind, source, pair, step).wait()
            return carry

        lax.fori_loop(0, half, run, 0)

        def add(step, carry):
            mid[step] = (
                source[2 * step + parity].astype(f32) + pair[step].astype(f32)
            ).astype(b16)
            return carry

        lax.fori_loop(0, half, add, 0)
        begin(line_copy, kind, mid, land, half)

    def end_line(kind, source, pair, mid, land, result):
        finish(line_copy, kind, mid, land, half)
        total = source[my_shard].astype(f32) + pair[place].astype(f32)
        for step in range(half - 1):
            total = total + land[step].astype(f32)
        result[...] = total

    def begin(copy, kind, source, target, count):
        def run(step, carry):
            copy(kind, source, target, step).start()
            return carry

        lax.fori_loop(1, count, run, 0)

    def finish(copy, kind, source, target, count):
        def run(step, carry):
            copy(kind, source, target, step).wait()
            return carry

        lax.fori_loop(1, count, run, 0)

    norm2_move = (tensor_copy, 0, lambda p: norm2_ref.at[p], lambda t: norm2_land.at[t - 1], groups)
    feed_move = (tensor_copy, 1, lambda p: feed_ref.at[p], lambda t: feed_land.at[t - 1], groups)
    rows_move = (tensor_copy, 2, lambda p: rows16, lambda t: rows_all.at[my_group], groups)
    norm1_move = (tensor_copy, 3, lambda p: norm1_part.at[p], lambda t: norm1_land.at[t - 1], groups)
    vector_move = (tensor_copy, 4, lambda p: vector_part, lambda t: vector_land.at[t - 1], groups)
    far_move = (dp_copy, 0, lambda p: vector_own.at[p], vector_far, shards)

    def total_of(own, land, count):
        total = own.astype(f32)
        for step in range(count - 1):
            total = total + land[step].astype(f32)
        return total

    begin(*norm2_move)
    begin_pair(0, reduce_ref, reduce_pair)
    begin(*feed_move)
    vector_part[...] = jnp.zeros_like(vector_part)
    finish(*norm2_move)
    grad_norm2 = total_of(norm2_ref[my_group], norm2_land, groups)
    back2, gain_row, shift_row = norm_back_rows(
        grad_norm2, normed2_ref[...], recip2_ref[...], gain2_ref[...]
    )
    grad_y = grad_y_ref[...]
    grad_rows = grad_y + back2
    rows16[...] = grad_rows.astype(b16)
    begin(*rows_move)
    input_out[...] = grad_rows
    rows_all[my_group] = grad_rows.astype(b16)
    width = grad_y.shape[1]
    vector_part[2:3, :width] = jnp.sum(grad_rows, axis=0, keepdims=True)
    vector_part[3:4, :width] = gain_row
    vector_part[4:5, :width] = shift_row
    vector_part[5:6, :width] = jnp.sum(grad_y, axis=0, keepdims=True)
    vector_part[6:7, : expand_bias_ref.shape[1]] = expand_bias_ref[...]
    finish(*feed_move)
    feed_rows = total_of(feed_ref[my_group], feed_land, groups)
    block_out[...] = live_ref[...] * (hidden_ref[...] + feed_rows + reduce_bias_ref[...])
    finish(*rows_move)
    begin_pair(1, expand_ref, expand_pair)
    share = rows_all.shape[1]
    rows = groups * share
    hidden16 = rows_all[...].reshape(rows, width)
    grad_att = across(hidden16, output_weight_ref[...], 1, 1).astype(b16)
    scale = HEAD_DIM ** (-0.5)
    span = heads * HEAD_DIM
    for head in range(heads):
        low = head * HEAD_DIM
        high = low + HEAD_DIM
        first = 3 * low
        att = grad_att[:, low:high]
        second = first + HEAD_DIM
        third = second + HEAD_DIM
        keys = jnp.concatenate([prior_ref[:, second:third], mixed_ref[:, second:third]], axis=0)
        values = jnp.concatenate(
            [prior_ref[:, third : third + HEAD_DIM], mixed_ref[:, third : third + HEAD_DIM]], axis=0
        )
        soft = soft_ref[head]
        grad_soft = across(att, values, 1, 1)
        delta = jnp.sum(soft * grad_soft, axis=-1, keepdims=True)
        grad_scores = (scale * soft * (grad_soft - delta)).astype(b16)
        grad_keys = across(grad_scores, mixed_ref[:, first:second], 0, 0)
        grad_values = across(soft.astype(b16), att, 0, 0)
        back_own[:, low:high] = grad_keys[:rows].astype(b16)
        back_own[:, span + low : span + high] = grad_values[:rows].astype(b16)
        mixed_grad[:, first : first + HEAD_DIM] = across(grad_scores, keys, 1, 0)
        mixed_grad[:, first + HEAD_DIM : first + 2 * HEAD_DIM] = grad_keys[rows:]
        mixed_grad[:, first + 2 * HEAD_DIM : first + 3 * HEAD_DIM] = grad_values[rows:]

    back_copy = pltpu.make_async_remote_copy(
        src_ref=back_own,
        dst_ref=back_land,
        send_sem=back_send,
        recv_sem=back_recv,
        device_id={"dp": lax.rem(my_shard + shards - 1, shards)},
        device_id_type=mesh_id,
    )

    @pl.when(my_shard > 0)
    def _():
        back_copy.start()

    begin_line(0, reduce_ref, reduce_pair, reduce_mid, reduce_land)
    output_grad = across(hidden16, attended_ref[...], 0, 0)
    piece = output_part.shape[1]
    for part in range(shards):
        output_part[part] = output_grad[part * piece : (part + 1) * piece].astype(b16)
    begin_pair(2, output_part, output_pair)

    @pl.when(my_shard < shards - 1)
    def _():
        back_copy.wait_recv()

    @pl.when(my_shard == shards - 1)
    def _():
        back_land[...] = jnp.zeros_like(back_land)

    for head in range(heads):
        low = head * HEAD_DIM
        high = low + HEAD_DIM
        key_at = 3 * low + HEAD_DIM
        value_at = key_at + HEAD_DIM
        mixed_grad[:, key_at:value_at] += back_land[:, low:high].astype(f32)
        mixed_grad[:, value_at : value_at + HEAD_DIM] += back_land[
            :, span + low : span + high
        ].astype(f32)
    mixed = mixed_grad[...]
    mixed16 = mixed.astype(b16)
    norm1 = across(mixed16, input_weight_ref[...], 1, 1).astype(b16)
    norm1_part[...] = norm1.reshape(groups, share, width)
    begin(*norm1_move)
    input_grad = across(first_in_ref[...], mixed16, 0, 0)
    for part in range(shards):
        input_part[part] = input_grad[part * piece : (part + 1) * piece].astype(b16)
    begin_pair(3, input_part, input_pair)
    begin_line(1, expand_ref, expand_pair, expand_mid, expand_land)
    bias_row = jnp.sum(mixed, axis=0, keepdims=True)
    for head in range(heads):
        first = 3 * head * HEAD_DIM
        goes = 2 * head * HEAD_DIM
        vector_part[7:8, goes : goes + HEAD_DIM] = bias_row[:, first : first + HEAD_DIM]
        vector_part[7:8, goes + HEAD_DIM : goes + 2 * HEAD_DIM] = bias_row[
            :, first + 2 * HEAD_DIM : first + 3 * HEAD_DIM
        ]
    finish(*norm1_move)
    begin_line(2, output_part, output_pair, output_mid, output_land)
    grad_norm1 = total_of(norm1_part[my_group], norm1_land, groups)
    back1, gain_row, shift_row = norm_back_rows(
        grad_norm1, normed1_ref[...], recip1_ref[...], gain1_ref[...]
    )
    vector_part[0:1, :width] = gain_row
    vector_part[1:2, :width] = shift_row
    begin(*vector_move)
    input_out[...] += back1
    finish(*vector_move)
    own = vector_part[...]
    added = vector_land[0]
    for step in range(1, groups - 1):
        added = added + vector_land[step]
    row_index = lax.broadcasted_iota(jnp.int32, own.shape, 0)
    own = own + jnp.where(row_index < 6, added, 0.0)
    narrow = 2 * span // shards
    for part in range(shards):
        vector_own[part] = own[:, part * piece : (part + 1) * piece]
        vector_own[part, 7:8, :narrow] = own[7:8, part * narrow : (part + 1) * narrow]
    begin(*far_move)
    begin_line(3, input_part, input_pair, input_mid, input_land)

    @pl.when(my_shard > 0)
    def _():
        back_copy.wait_send()

    end_line(0, reduce_ref, reduce_pair, reduce_mid, reduce_land, reduce_sum)
    end_line(1, expand_ref, expand_pair, expand_mid, expand_land, expand_sum)
    end_line(2, output_part, output_pair, output_mid, output_land, output_sum)
    finish(*far_move)
    vector_sum[...] = total_of(vector_own[my_shard], vector_far, shards)
    end_line(3, input_part, input_pair, input_mid, input_land, input_sum)


def tail(shards, groups, heads, operands):
    f32 = jnp.float32
    b16 = jnp.bfloat16
    share, width = operands[4].shape
    rows = share * groups
    piece = operands[2].shape[1]
    hidden = operands[2].shape[2]
    span = heads * HEAD_DIM
    broad = max(width, hidden, 3 * span)
    half = shards // 2
    sizes = (hidden, hidden, span, 3 * span)
    vmem = pl.BlockSpec(memory_space=pltpu.VMEM)

    def shape(*sizes):
        return jax.ShapeDtypeStruct(sizes, f32)

    dma = pltpu.SemaphoreType.DMA
    return pl.pallas_call(
        functools.partial(tail_kernel, shards, groups, heads),
        out_shape=[
            shape(share, width),
            shape(share, width),
            shape(piece, 3 * span),
            shape(piece, span),
            shape(piece, hidden),
            shape(piece, hidden),
            shape(8, piece),
        ],
        in_specs=[vmem] * len(operands),
        out_specs=[vmem] * 7,
        scratch_shapes=[
            pltpu.VMEM((groups - 1, share, width), b16),
            pltpu.VMEM((groups - 1, share, width), b16),
            pltpu.VMEM((share, width), b16),
            pltpu.VMEM((groups, share, width), b16),
            pltpu.VMEM((groups, share, width), b16),
            pltpu.VMEM((groups - 1, share, width), b16),
            pltpu.VMEM((8, broad), f32),
            pltpu.VMEM((groups - 1, 8, broad), f32),
            pltpu.VMEM((shards, 8, piece), f32),
            pltpu.VMEM((shards - 1, 8, piece), f32),
            pltpu.VMEM((rows, 2 * span), b16),
            pltpu.VMEM((rows, 2 * span), b16),
            pltpu.VMEM((rows, 3 * span), f32),
            pltpu.VMEM((shards, piece, span), b16),
            pltpu.VMEM((shards, piece, 3 * span), b16),
            *[pltpu.VMEM((half, piece, size), b16) for size in sizes],
            *[pltpu.VMEM((half, piece, size), b16) for size in sizes],
            *[pltpu.VMEM((half - 1, piece, size), b16) for size in sizes],
            dma((5, groups - 1)),
            dma((5, groups - 1)),
            dma((4, half)),
            dma((4, half)),
            dma((4, half - 1)),
            dma((4, half - 1)),
            dma((shards - 1,)),
            dma((shards - 1,)),
            dma,
            dma,
        ],
        compiler_params=pltpu.CompilerParams(
            collective_id=2, has_side_effects=True, vmem_limit_bytes=48 * 1024 * 1024
        ),
    )(*operands)


def layer_norm(values_in, gain_row, shift_row):
    centred = values_in - jnp.mean(values_in, axis=-1, keepdims=True)
    reciprocal = lax.rsqrt(jnp.mean(centred * centred, axis=-1, keepdims=True) + EPSILON)
    normed = centred * reciprocal
    return (normed * gain_row + shift_row, normed, reciprocal)


def gelu_parts(pre_act):
    tanh_value = jnp.tanh(GELU_COEF * (pre_act + CUBIC * pre_act * pre_act * pre_act))
    result = 0.5 * pre_act * (1.0 + tanh_value)
    slope_value = 0.5 * (1.0 + tanh_value) + 0.5 * pre_act * (
        1.0 - tanh_value * tanh_value
    ) * GELU_COEF * (1.0 + 3.0 * CUBIC * pre_act * pre_act)
    return (result, slope_value)


def full_bias(pairs, group_heads):
    shaped = pairs.reshape(group_heads, 2, HEAD_DIM)
    return jnp.stack([shaped[:, 0], jnp.zeros_like(shaped[:, 0]), shaped[:, 1]], axis=1).reshape(
        group_heads * 3 * HEAD_DIM
    )


def per_device(
    block_input,
    first_gain,
    first_shift,
    input_weight,
    input_bias,
    output_weight,
    output_bias,
    second_gain,
    second_shift,
    expand_weight,
    expand_bias,
    reduce_weight,
    reduce_bias,
    output_grad,
    segment_ids,
    shard_counts,
):
    f32 = jnp.float32
    b16 = jnp.bfloat16
    block_rows = block_input.shape[0]
    group_heads = output_weight.shape[0] // HEAD_DIM
    group_width = group_heads * HEAD_DIM
    tensor_count = lax.axis_size("tensor")
    share_rows = block_rows // tensor_count
    row_start = lax.axis_index("tensor") * share_rows

    def own_rows(values):
        return lax.dynamic_slice_in_dim(values, row_start, share_rows, 0)

    shard_index = lax.axis_index("dp")
    prior_index = jnp.maximum(shard_index - 1, 0)
    position = jnp.arange(block_rows, dtype=jnp.int32)
    own_ids = lax.dynamic_slice_in_dim(segment_ids, shard_index * block_rows, block_rows)
    prior_ids = lax.dynamic_slice_in_dim(segment_ids, prior_index * block_rows, block_rows)
    own_live = position < shard_counts[shard_index]
    prior_live = (position < shard_counts[prior_index]) & (shard_index > 0)
    diagonal = position[None, :] == position[:, None]
    same_own = (
        (own_ids[:, None] == own_ids[None, :])
        & (position[None, :] <= position[:, None])
        & (own_live[None, :] | diagonal)
    )
    same_prior = (own_ids[:, None] == prior_ids[None, :]) & prior_live[None, :]
    allowed = jnp.concatenate([same_prior, same_own], axis=1)
    live_col = own_live.astype(f32)[:, None]
    first_out, normed1, recip1 = layer_norm(block_input, first_gain, first_shift)
    first_in = first_out.astype(b16)
    mixed = jnp.dot(first_in, input_weight, preferred_element_type=f32) + full_bias(
        input_bias, group_heads
    )
    mixed16 = mixed.astype(b16)
    prior_mixed = from_behind(mixed16, "dp", 1)
    attended, soft = attention(group_heads, mixed16, prior_mixed, allowed.astype(f32))
    in_shares = (tensor_count, share_rows, block_input.shape[1])
    (mixed_rows,) = scatter_sum(
        [jnp.dot(attended, output_weight, preferred_element_type=f32).astype(b16).reshape(in_shares)],
        "tensor",
        0,
    )
    hidden_rows = own_rows(block_input) + mixed_rows + output_bias
    second_out, normed2, recip2 = layer_norm(hidden_rows, second_gain, second_shift)
    second_in = gather(second_out.astype(b16), "tensor", tensor_count, 1).reshape(block_input.shape)
    pre_act = jnp.dot(second_in, expand_weight, preferred_element_type=f32) + expand_bias
    activ, gelu_slope = gelu_parts(pre_act)
    activated = activ.astype(b16)
    feed_part = jnp.dot(activated, reduce_weight, preferred_element_type=f32)
    grad_y = live_col * output_grad
    grad_y16 = grad_y.astype(b16)
    grad_pre = (
        jnp.einsum("rd,kd->rk", grad_y16, reduce_weight, preferred_element_type=f32) * gelu_slope
    )
    grad_pre16 = grad_pre.astype(b16)
    expand_bias_grad = jnp.sum(grad_pre, axis=0)
    norm2_part = jnp.einsum("rk,dk->rd", grad_pre16, expand_weight, preferred_element_type=f32)
    shard_count = lax.axis_size("dp")
    expand_weight_grad = jnp.einsum("rd,rk->dk", second_in, grad_pre16, preferred_element_type=f32)
    reduce_weight_grad = jnp.einsum("rd,rk->dk", grad_y16, activated, preferred_element_type=f32)

    def pieces(value):
        return value.reshape(shard_count, value.shape[0] // shard_count, value.shape[1])

    block_output, input_grad, input_sum, output_sum, expand_sum, reduce_sum, vectors = tail(
        shard_count,
        tensor_count,
        group_heads,
        [
            feed_part.astype(b16).reshape(in_shares),
            norm2_part.astype(b16).reshape(in_shares),
            pieces(expand_weight_grad.astype(b16)),
            pieces(reduce_weight_grad.astype(b16)),
            hidden_rows,
            normed2,
            recip2,
            second_gain[None],
            reduce_bias[None],
            own_rows(grad_y),
            own_rows(live_col),
            expand_bias_grad[None],
            attended,
            output_weight,
            mixed16,
            prior_mixed,
            soft,
            first_in,
            input_weight,
            own_rows(normed1),
            own_rows(recip1),
            first_gain[None],
        ],
    )
    return (
        block_output,
        input_grad,
        vectors[0],
        vectors[1],
        input_sum,
        vectors[7, : input_bias.shape[0] // shard_count],
        output_sum.T,
        vectors[2],
        vectors[3],
        vectors[4],
        expand_sum,
        vectors[6],
        reduce_sum.T,
        vectors[5],
    )


def solution(mesh):
    placed = (
        P("dp", None),
        P(),
        P(),
        P(None, "tensor"),
        P("tensor"),
        P("tensor", None),
        P(),
        P(),
        P(),
        P(None, "tensor"),
        P("tensor"),
        P("tensor", None),
        P(),
        P("dp", None),
        P(),
        P(),
    )
    return jax.shard_map(
        per_device,
        mesh=mesh,
        in_specs=placed,
        out_specs=(
            P(("dp", "tensor"), None),
            P(("dp", "tensor"), None),
            P("dp"),
            P("dp"),
            P("dp", "tensor"),
            P(("tensor", "dp")),
            P("tensor", "dp"),
            P("dp"),
            P("dp"),
            P("dp"),
            P("dp", "tensor"),
            P(("tensor", "dp")),
            P("tensor", "dp"),
            P("dp"),
        ),
        check_vma=False,
    )
```
